1024 devices in a mesh: ga: 128 (over y, z), band: 8 (over x, core).
Axes of the slice: x: 4, y: 8, z: 16, core: 2. Of those that a mesh axis runs over, the one named last changes fastest.
Arguments:
- band_coeffs: bfloat16 [131072, 512], P('ga', 'band'), may hold values from -6 to 6
- beta_vectors: bfloat16 [131072, 2048], P('ga'), may hold values from -0.015625 to 0.015625
- atomic_waves: bfloat16 [131072, 1280], P('ga'), may hold values from -0.015625 to 0.015625
- beta_coupling: float32 [2048, 11], replicated, may hold values from -1 to 2
- ortho_inverse: bfloat16 [1280, 1280], replicated, may hold values from -1 to 2
- hubbard_energy: float32 [3], replicated, may hold values from 1 to 4
- band_weight: float32 [512], P('band'), may hold values from 0 to 0.0078125
- orbital_start: int32 [1280], replicated, may hold values from 0 to 1277, as said below
- orbital_species: int32 [1280], replicated, may hold values from 0 to 2, as said below
- beta_start: int32 [2048], replicated, may hold values from 0 to 2046, as said below
Outputs:
- hubbard_apply: bfloat16 [131072, 512], P('ga', 'band')
The draws below stay inside these ranges and needn't reach their ends.
Inputs may be any that keep to these rules, and one draw needn't show every extreme that they name: `orbital_start`: every atom holds 3 or 5 consecutive orbitals; each orbital holds the index of its atom's first orbital. `orbital_species`: orbitals of 5-orbital atoms have species 0 or 1, orbitals of 3-orbital atoms species 2. `beta_start`: every atom holds 2 or 6 consecutive projectors; each projector holds the index of its atom's first projector.
All inputs are finite; a program needn't handle non-finite values.
Results may differ from the reference program's by a relative error of at most 0.0085.
Values sent between devices are 32-bit elements; how exact they have to be, the bound alone decides.
A program may use at most 32 MiB of HBM per device.

```python
import jax
import jax.numpy as jnp
from jax import lax

NWFC = 1280
NBETA = 2048
ORB_REACH = 4
BETA_REACH = 5
NSPEC = 3
NPW = 131072
NBANDS = 512


def orbital_layout(key):
    groups = NWFC // 8
    flips = jax.random.randint(jax.random.fold_in(key, 11), (groups,), 0, 2)
    metals = jax.random.randint(jax.random.fold_in(key, 12), (groups,), 0, 2)
    first_size = jnp.where(flips == 0, 5, 3)
    place = jnp.arange(8, dtype=jnp.int32)[None, :]
    in_first = place < first_size[:, None]
    local = jnp.where(in_first, 0, first_size[:, None])
    starts = (jnp.arange(groups, dtype=jnp.int32) * 8)[:, None] + local
    own_size = jnp.where(in_first, first_size[:, None], 8 - first_size[:, None])
    species = jnp.where(own_size == 5, metals[:, None], 2)
    return (starts.reshape(-1).astype(jnp.int32), species.reshape(-1).astype(jnp.int32))


def draw_orbital_start(key, part):
    return orbital_layout(key)[0]


def draw_orbital_species(key, part):
    return orbital_layout(key)[1]


def draw_beta_start(key, part):
    groups = NBETA // 8
    flips = jax.random.randint(jax.random.fold_in(key, 21), (groups,), 0, 2)
    first_size = jnp.where(flips == 0, 6, 2)
    place = jnp.arange(8, dtype=jnp.int32)[None, :]
    local = jnp.where(place < first_size[:, None], 0, first_size[:, None])
    starts = (jnp.arange(groups, dtype=jnp.int32) * 8)[:, None] + local
    return starts.reshape(-1).astype(jnp.int32)


def draw_ortho_inverse(key, part):
    noise = jax.random.normal(jax.random.fold_in(key, 31), (NWFC, NWFC), jnp.float32)
    spread = 0.0085
    diagonal = jnp.ones((NWFC,), jnp.float32)
    return (jnp.diag(diagonal) + spread * (noise + noise.T) / 1.4142135).astype(jnp.bfloat16)


def draw_band_weight(key, part):
    position = jnp.arange(NBANDS, dtype=jnp.float32) / NBANDS
    factor = jax.random.uniform(jax.random.fold_in(key, 41), (NBANDS,), jnp.float32, 0.5, 1.0)
    return (4.0 - 3.0 * position) * factor / NBANDS


def levels(rng, dims, split, smallest, high):
    gain = 1.0
    for dim, shards_of in split:
        steps = jax.random.uniform(jax.random.fold_in(jax.random.fold_in(rng, 6), dim), (shards_of,), jnp.float32, smallest / len(split), high / len(split))
        gain = gain * jnp.repeat(jnp.exp(steps), dims[dim] // shards_of).reshape((-1,) + (1,) * (len(dims) - 1 - dim))
    return gain


def centred(stream_key, shape, scale, most, shards=(), kind=jnp.bfloat16):
    array = scale * jax.random.normal(stream_key, shape, jnp.float32)
    if shards:
        array = array * levels(stream_key, shape, shards, -0.22, 0.18)
    return jnp.clip(array, -most, most).astype(kind)


def setup_inputs(seed: int = 0) -> dict:
    keys = jax.random.split(jax.random.key(seed), 11)
    return {
        "band_coeffs": centred(keys[0], (NPW, NBANDS), 1.0, 6.0, ((0, 128), (1, 8))),
        "beta_vectors": centred(keys[1], (NPW, NBETA), NPW ** -0.5, 0.015625, ((0, 128),)),
        "atomic_waves": centred(keys[2], (NPW, NWFC), NPW ** -0.5, 0.015625, ((0, 128),)),
        "beta_coupling": jnp.clip(jax.random.uniform(keys[3], (NBETA, 2 * BETA_REACH + 1), jnp.float32, -1.0, 2.0), -1.0, 2.0),
        "ortho_inverse": draw_ortho_inverse(jax.random.fold_in(keys[10], 71), 0),
        "hubbard_energy": jnp.clip(jax.random.uniform(keys[5], (NSPEC,), jnp.float32, 1.0, 4.0), 1.0, 4.0),
        "band_weight": draw_band_weight(jax.random.fold_in(keys[10], 71), 0),
        "orbital_start": draw_orbital_start(jax.random.fold_in(keys[10], 71), 0),
        "orbital_species": draw_orbital_species(jax.random.fold_in(keys[10], 71), 0),
        "beta_start": draw_beta_start(jax.random.fold_in(keys[10], 71), 0),
    }


def rim_shift(extended, reach, offset, rows):
    return lax.slice_in_dim(extended, reach + offset, reach + offset + rows, axis=0)


def same_atom(start_ext, reach, rows):
    centre = rim_shift(start_ext, reach, 0, rows)
    return jnp.stack([(rim_shift(start_ext, reach, offset, rows) == centre).astype(jnp.float32) for offset in range(-reach, reach + 1)])


def band_apply(coupling, extended, reach, rows):
    total = jnp.zeros((rows, extended.shape[1]), jnp.float32)
    for offset in range(-reach, reach + 1):
        total = total + coupling[offset + reach][:, None] * rim_shift(extended, reach, offset, rows)
    return total


def beta_matrix(beta_coupling, beta_start):
    rows = beta_start.shape[0]
    start_ext = jnp.pad(beta_start, BETA_REACH, constant_values=-1)
    mask = same_atom(start_ext, BETA_REACH, rows)
    padded = jnp.pad(beta_coupling, ((BETA_REACH, BETA_REACH), (0, 0)))
    terms = []
    for offset in range(-BETA_REACH, BETA_REACH + 1):
        mirror = rim_shift(padded, BETA_REACH, offset, rows)[:, BETA_REACH - offset]
        terms.append(0.5 * (beta_coupling[:, BETA_REACH + offset] + mirror))
    return jnp.stack(terms) * mask


def occupancy(extended, weights, mask, reach, rows):
    centre = rim_shift(extended, reach, 0, rows)
    weighted = centre * weights[None, :]
    return jnp.stack([jnp.sum(weighted * rim_shift(extended, reach, offset, rows), axis=1) for offset in range(-reach, reach + 1)]) * mask


def hubbard_mix(occupied, u_rows, mask, extended, reach, rows):
    centre_flag = (jnp.arange(2 * reach + 1) == reach).astype(jnp.float32)[:, None]
    potential = u_rows[None, :] * (0.5 * centre_flag - occupied) * mask
    return band_apply(potential, extended, reach, rows)


def per_orbital_u(species, hubbard_energy):
    onehot = (species[:, None] == jnp.arange(NSPEC)[None, :]).astype(jnp.float32)
    return jnp.dot(onehot, hubbard_energy, precision=lax.Precision.HIGHEST)


def reference(band_coeffs, beta_vectors, atomic_waves, beta_coupling, ortho_inverse, hubbard_energy, band_weight, orbital_start, orbital_species, beta_start):
    highest = lax.Precision.HIGHEST
    ortho_full = ortho_inverse.astype(jnp.float32)
    coupling = beta_matrix(beta_coupling, beta_start)
    beta_correlation = jnp.dot(beta_vectors.T, band_coeffs, preferred_element_type=jnp.float32)
    corrected = band_apply(coupling, jnp.pad(beta_correlation, ((BETA_REACH, BETA_REACH), (0, 0))), BETA_REACH, NBETA).astype(jnp.bfloat16)
    correlation_psi = (band_coeffs.astype(jnp.float32) + jnp.dot(beta_vectors, corrected, preferred_element_type=jnp.float32)).astype(jnp.bfloat16)
    partial_sums = jnp.dot(atomic_waves.T, correlation_psi, preferred_element_type=jnp.float32)
    projections = jnp.dot(ortho_full, partial_sums, precision=highest)
    extended = jnp.pad(projections, ((ORB_REACH, ORB_REACH), (0, 0)))
    start_ext = jnp.pad(orbital_start, ORB_REACH, constant_values=-1)
    mask = same_atom(start_ext, ORB_REACH, NWFC)
    occupied = occupancy(extended, band_weight, mask, ORB_REACH, NWFC)
    u_full = per_orbital_u(orbital_species, hubbard_energy)
    mixed = hubbard_mix(occupied, u_full, mask, extended, ORB_REACH, NWFC)
    rotated = jnp.dot(ortho_full, mixed, precision=highest).astype(jnp.bfloat16)
    hubbard_waves = jnp.dot(atomic_waves, rotated, preferred_element_type=jnp.float32)
    wave_half = hubbard_waves.astype(jnp.bfloat16)
    beta_update = jnp.dot(beta_vectors.T, wave_half, preferred_element_type=jnp.float32)
    correction = band_apply(coupling, jnp.pad(beta_update, ((BETA_REACH, BETA_REACH), (0, 0))), BETA_REACH, NBETA).astype(jnp.bfloat16)
    return (hubbard_waves + jnp.dot(beta_vectors, correction, preferred_element_type=jnp.float32)).astype(jnp.bfloat16)
```

```python
import functools

import jax
import jax.numpy as jnp
from jax import lax
from jax.experimental import pallas as pl
from jax.experimental.pallas import tpu as pltpu
from jax.sharding import PartitionSpec as P

ORB_REACH = 4
BETA_REACH = 5
NY = 8
NZ = 16
HALVES = 1
MESH = pl.DeviceIdType.MESH
F32 = jnp.float32
BF16 = jnp.bfloat16


def dot_nn(a, b):
    return jnp.dot(a, b, preferred_element_type=F32)


def dot_nt(a, b):
    return lax.dot_general(a, b, (((1,), (1,)), ((), ())), preferred_element_type=F32)


def ahead(x, k):
    n = x.shape[1]
    return x if k % n == 0 else pltpu.roll(x, (-k) % n, 1)


def order(n):
    return sorted(range(1, n), key=lambda d: -min(d, n - d))


def wait_bytes(ref, sem):
    pltpu.make_async_copy(ref, ref, sem).wait()


class RingSum:
    def __init__(self, src, dst, row0, rows, y_in, z_in, mine, recv, send, y, z, band):
        self.src, self.dst = src, dst
        self.lanes = src.shape[1]
        self.split = NY * 8 // rows
        self.width = self.lanes // self.split
        self.tiles = self.width // 128
        self.stride = NZ // self.tiles
        self.row0 = row0
        self.y_in, self.z_in, self.mine = y_in, z_in, mine
        self.recv, self.send = recv, send
        self.y, self.z, self.band = y, z, band

    def rows_of(self, y):
        return pl.ds(pl.multiple_of(self.row0 + (y // self.split) * 8, 8), 8)

    def lanes_of(self, y):
        if self.split == 1:
            return pl.ds(0, self.width)
        return pl.ds(pl.multiple_of((y % self.split) * self.width, 128), self.width)

    def tile_lanes(self, y, tile):
        base = (y % self.split) * self.width if self.split > 1 else 0
        return pl.ds(pl.multiple_of(base + tile * 128, 128), 128)

    def owns(self, z):
        ok = z // self.stride < self.tiles
        if self.stride > 1:
            ok = jnp.logical_and(ok, z % self.stride == 0)
        return ok

    def all_own(self):
        return self.tiles == NZ

    def copy(self, src, dst, phase, y, z):
        pltpu.make_async_remote_copy(
            src_ref=src,
            dst_ref=dst,
            send_sem=self.send.at[phase],
            recv_sem=self.recv.at[phase],
            device_id=(y * NZ + z, self.band),
            device_id_type=MESH,
        ).start()

    def start(self):
        for d in order(NY):
            to = (self.y + d) % NY
            self.copy(self.src.at[self.rows_of(to), self.lanes_of(to)], self.y_in.at[d - 1], 0, to, self.z)

    def when(self, cond, body):
        if self.all_own():
            body()
        else:
            pl.when(cond)(body)

    def second(self):
        wait_bytes(self.y_in, self.recv.at[0])
        total = self.src[self.rows_of(self.y), self.lanes_of(self.y)]
        for d in range(NY - 1):
            total = total + self.y_in[d]
        self.mine[...] = total
        for d in order(NZ):
            to = (self.z + d) % NZ
            tile = to // self.stride

            def go(to=to, tile=tile, d=d):
                lanes = pl.ds(pl.multiple_of(tile * 128, 128), 128)
                self.copy(self.mine.at[:, lanes], self.z_in.at[d - 1], 1, self.y, to)

            self.when(self.owns(to), go)

    def third(self):
        def go():
            wait_bytes(self.z_in, self.recv.at[1])
            tile = self.z // self.stride
            total = self.mine[:, pl.ds(pl.multiple_of(tile * 128, 128), 128)]
            for d in range(NZ - 1):
                total = total + self.z_in[d]
            here = (self.rows_of(self.y), self.tile_lanes(self.y, tile))
            self.dst[here] = total
            for d in order(NZ):
                to = (self.z + d) % NZ
                self.copy(self.dst.at[here], self.dst.at[here], 2, self.y, to)

        self.when(self.owns(self.z), go)

    def z_wait(self, sem):
        if self.all_own():
            wait_bytes(self.z_in, sem)
        else:
            own = self.owns(self.z)
            pl.when(own)(lambda: wait_bytes(self.z_in.at[pl.ds(0, self.tiles - 1)], sem))
            pl.when(jnp.logical_not(own))(lambda: wait_bytes(self.z_in.at[pl.ds(0, self.tiles)], sem))

    def fourth(self):
        self.z_wait(self.recv.at[2])
        here = (self.rows_of(self.y), self.lanes_of(self.y))
        for d in order(NY):
            to = (self.y + d) % NY
            self.copy(self.dst.at[here], self.dst.at[here], 3, to, self.z)

    def finish(self):
        wait_bytes(self.y_in, self.recv.at[3])

    def drain(self):
        wait_bytes(self.y_in, self.send.at[0])
        self.z_wait(self.send.at[1])
        self.when(self.owns(self.z), lambda: wait_bytes(self.z_in, self.send.at[2]))
        wait_bytes(self.y_in, self.send.at[3])


def split3(x):
    high = x.astype(BF16)
    rest = x - high.astype(F32)
    mid = rest.astype(BF16)
    low = (rest - mid.astype(F32)).astype(BF16)
    return jnp.concatenate([high, mid, low], axis=0)


def kernel(
    psi_hbm, beta_hbm, atom_hbm, ortho_hbm, coup_in, energy, weight_in, ostart, ospec, bstart, out,
    psi, beta, atom, ortho, coup, orb, wcol, wb, wo, fb, fo, half_b, half_o, hw, cpsi, pot,
    occ_mine, occ_in, yb_in, yo_in, z_in, mine_b, mine_o, load_sem, recv, send, occ_sem,
):
    bands, npw = psi.shape
    nbeta, norb = beta.shape[1], atom.shape[1]
    rows = bands // HALVES
    g = lax.axis_index("ga")
    band = lax.axis_index("band")
    y, z = g // NZ, g % NZ
    nband = 8
    step = 512

    loads = [pltpu.make_async_copy(psi_hbm, psi, load_sem.at[0])]
    for j in range(nbeta // step):
        cols = pl.ds(j * step, step)
        loads.append(pltpu.make_async_copy(beta_hbm.at[:, cols], beta.at[:, cols], load_sem.at[1 + j]))
    late = [
        pltpu.make_async_copy(atom_hbm, atom, load_sem.at[5]),
        pltpu.make_async_copy(ortho_hbm, ortho, load_sem.at[6]),
    ]
    for c in loads + late:
        c.start()

    barrier = pltpu.get_barrier_semaphore()
    for d in order(NZ):
        pl.semaphore_signal(barrier, inc=1, device_id=(y * NZ + (z + d) % NZ, band), device_id_type=MESH)
    for d in order(NY):
        pl.semaphore_signal(barrier, inc=1, device_id=(((y + d) % NY) * NZ + z, band), device_id_type=MESH)
    for d in range(1, nband):
        pl.semaphore_signal(barrier, inc=1, device_id=(g, (band + d) % nband), device_id_type=MESH)

    def ring(which, h):
        i = which * HALVES + h
        if which == 1:
            src, dst, y_in, mine = wo, fo, yo_in.at[h], mine_o.at[h]
        else:
            n = (which // 2) * HALVES + h
            src, dst, y_in, mine = wb.at[which // 2], fb.at[which // 2], yb_in.at[n], mine_b.at[n]
        return RingSum(src, dst, h * rows, rows, y_in, z_in.at[i], mine, recv.at[i], send.at[i], y, z, band)

    sums = [[ring(w, h) for h in range(HALVES)] for w in range(3)]
    halves = range(HALVES)
    part = [pl.ds(h * rows, rows) for h in halves]

    loads[0].wait()
    for h in halves:
        for j in range(nbeta // step):
            if h == 0:
                loads[1 + j].wait()
            cols = pl.ds(j * step, step)
            wb[0, part[h], cols] = dot_nn(psi[part[h], :], beta[:, cols])
        if h == 0:
            pl.semaphore_wait(barrier, NZ - 1 + NY - 1 + nband - 1)
        sums[0][h].start()

    place = lax.broadcasted_iota(jnp.int32, (1, nbeta), 1)
    first = bstart[...]
    for k in range(-BETA_REACH, BETA_REACH + 1):
        there = jnp.logical_and(place + k >= 0, place + k < nbeta)
        same = jnp.logical_and(ahead(first, k) == first, there)
        mirror = ahead(coup_in[BETA_REACH - k : BETA_REACH - k + 1, :], k)
        value = 0.5 * (coup_in[BETA_REACH + k : BETA_REACH + k + 1, :] + mirror)
        coup[BETA_REACH + k : BETA_REACH + k + 1, :] = jnp.where(same, value, 0.0)
    place = lax.broadcasted_iota(jnp.int32, (1, norb), 1)
    first = ostart[...]
    for k in range(-ORB_REACH, ORB_REACH + 1):
        there = jnp.logical_and(place + k >= 0, place + k < norb)
        same = jnp.logical_and(ahead(first, k) == first, there)
        orb[ORB_REACH + k : ORB_REACH + k + 1, :] = jnp.where(same, 1.0, 0.0)
    species = ospec[...]
    u = jnp.zeros((1, norb), F32)
    for s in range(3):
        u = u + jnp.where(species == s, energy[0, s], 0.0)
    orb[2 * ORB_REACH + 1 : 2 * ORB_REACH + 2, :] = u
    row = lax.broadcasted_iota(jnp.int32, (bands, bands), 0)
    col = lax.broadcasted_iota(jnp.int32, (bands, bands), 1)
    wcol[...] = jnp.sum(jnp.where(row == col, weight_in[...], 0.0), axis=1, keepdims=True)

    def apply_q(full, h):
        for i in range(rows // 16):
            pair = []
            for j in range(2):
                x = full[h * rows + i * 16 + j * 8 : h * rows + i * 16 + j * 8 + 8, :]
                total = coup[BETA_REACH : BETA_REACH + 1, :] * x
                for k in range(-BETA_REACH, BETA_REACH + 1):
                    if k != 0:
                        total = total + coup[BETA_REACH + k : BETA_REACH + k + 1, :] * ahead(x, k)
                pair.append(total)
            half_b[h * rows + i * 16 : h * rows + i * 16 + 16, :] = jnp.concatenate(pair, axis=0).astype(BF16)

    block = 256

    def middle(which):
        for name in ("second", "third", "fourth"):
            for h in halves:
                getattr(sums[which][h], name)()

    middle(0)
    for c in late:
        c.wait()
    for h in halves:
        sums[0][h].finish()
        apply_q(fb.at[0], h)
        for j in range(npw // block):
            cols = pl.ds(j * block, block)
            value = psi[part[h], cols].astype(F32) + dot_nt(half_b[part[h], :], beta[cols, :])
            cpsi[part[h], cols] = value.astype(BF16)
        for j in range(norb // block):
            cols = pl.ds(j * block, block)
            wo[part[h], cols] = dot_nn(cpsi[part[h], :], atom[:, cols])
        sums[1][h].start()

    middle(1)

    def times_ortho(x, h):
        stacked = split3(x)
        for j in range(norb // block):
            cols = pl.ds(j * block, block)
            y3 = dot_nt(stacked, ortho[cols, :])
            yield cols, y3[:rows] + y3[rows : 2 * rows] + y3[2 * rows :]

    accs = None
    for h in halves:
        sums[1][h].finish()
        for cols, value in times_ortho(fo[part[h], :], h):
            wo_proj = value
            pot[part[h], cols] = wo_proj
    for i in range(bands // 8):
        p = pot[i * 8 : i * 8 + 8, :]
        weighted = p * wcol[i * 8 : i * 8 + 8, :]
        terms = [weighted * ahead(p, k) for k in range(ORB_REACH + 1)]
        accs = terms if accs is None else [a + t for a, t in zip(accs, terms)]
    for k in range(ORB_REACH + 1):
        occ_mine[k : k + 1, :] = jnp.sum(accs[k], axis=0, keepdims=True)
    occ_mine[ORB_REACH + 1 :, :] = jnp.zeros((8 - ORB_REACH - 1, norb), F32)
    for d in range(1, nband):
        pltpu.make_async_remote_copy(
            src_ref=occ_mine,
            dst_ref=occ_in.at[d - 1],
            send_sem=occ_sem.at[0],
            recv_sem=occ_sem.at[1],
            device_id=(g, (band + d) % nband),
            device_id_type=MESH,
        ).start()
    wait_bytes(occ_in, occ_sem.at[1])
    occ = occ_mine[...]
    for d in range(nband - 1):
        occ = occ + occ_in[d]

    u = orb[2 * ORB_REACH + 1 : 2 * ORB_REACH + 2, :]
    potential = []
    for k in range(-ORB_REACH, ORB_REACH + 1):
        value = occ[abs(k) : abs(k) + 1, :]
        value = ahead(value, k) if k < 0 else value
        same = orb[ORB_REACH + k : ORB_REACH + k + 1, :]
        potential.append(u * ((0.5 if k == 0 else 0.0) - value * same) * same)

    for h in halves:
        mixed = []
        for i in range(rows // 8):
            x = pot[h * rows + i * 8 : h * rows + i * 8 + 8, :]
            total = potential[ORB_REACH] * x
            for k in range(-ORB_REACH, ORB_REACH + 1):
                if k != 0:
                    total = total + potential[ORB_REACH + k] * ahead(x, k)
            mixed.append(total)
        for cols, value in times_ortho(jnp.concatenate(mixed, axis=0), h):
            half_o[part[h], cols] = value.astype(BF16)
        for j in range(npw // block):
            cols = pl.ds(j * block, block)
            value = dot_nt(half_o[part[h], :], atom[cols, :])
            hw[part[h], cols] = value
            cpsi[part[h], cols] = value.astype(BF16)
        for j in range(nbeta // step):
            cols = pl.ds(j * step, step)
            wb[1, part[h], cols] = dot_nn(cpsi[part[h], :], beta[:, cols])
        sums[2][h].start()

    middle(2)
    for h in halves:
        sums[2][h].finish()
        apply_q(fb.at[1], h)
        for j in range(npw // block):
            cols = pl.ds(j * block, block)
            value = hw[part[h], cols] + dot_nt(half_b[part[h], :], beta[cols, :])
            out[part[h], cols] = value.astype(BF16)

    for w in range(3):
        for h in halves:
            sums[w][h].drain()
    wait_bytes(occ_in, occ_sem.at[0])


def shards(
    band_coeffs, beta_vectors, atomic_waves, beta_coupling, ortho_inverse, hubbard_energy, band_weight, orbital_start,
    orbital_species, beta_start,
):
    npw, bands = band_coeffs.shape
    nbeta, norb = beta_vectors.shape[1], atomic_waves.shape[1]
    rows = bands // HALVES
    wide_b, wide_o = nbeta * rows // (NY * 8), norb * rows // (NY * 8)
    hbm = pl.BlockSpec(memory_space=pl.ANY)
    vmem = pl.BlockSpec(memory_space=pltpu.VMEM)
    smem = pl.BlockSpec(memory_space=pltpu.SMEM)
    out = pl.pallas_call(
        kernel,
        out_shape=jax.ShapeDtypeStruct((bands, npw), BF16),
        in_specs=[hbm, hbm, hbm, hbm, vmem, smem, vmem, vmem, vmem, vmem],
        out_specs=vmem,
        scratch_shapes=[
            pltpu.VMEM((bands, npw), BF16),
            pltpu.VMEM((npw, nbeta), BF16),
            pltpu.VMEM((npw, norb), BF16),
            pltpu.VMEM((norb, norb), BF16),
            pltpu.VMEM((16, nbeta), F32),
            pltpu.VMEM((16, norb), F32),
            pltpu.VMEM((bands, 1), F32),
            pltpu.VMEM((2, bands, nbeta), F32),
            pltpu.VMEM((bands, norb), F32),
            pltpu.VMEM((2, bands, nbeta), F32),
            pltpu.VMEM((bands, norb), F32),
            pltpu.VMEM((bands, nbeta), BF16),
            pltpu.VMEM((bands, norb), BF16),
            pltpu.VMEM((bands, npw), F32),
            pltpu.VMEM((bands, npw), BF16),
            pltpu.VMEM((bands, norb), F32),
            pltpu.VMEM((8, norb), F32),
            pltpu.VMEM((7, 8, norb), F32),
            pltpu.VMEM((2 * HALVES, NY - 1, 8, wide_b), F32),
            pltpu.VMEM((HALVES, NY - 1, 8, wide_o), F32),
            pltpu.VMEM((3 * HALVES, NZ - 1, 8, 128), F32),
            pltpu.VMEM((2 * HALVES, 8, wide_b), F32),
            pltpu.VMEM((HALVES, 8, wide_o), F32),
            pltpu.SemaphoreType.DMA((7,)),
            pltpu.SemaphoreType.DMA((3 * HALVES, 4)),
            pltpu.SemaphoreType.DMA((3 * HALVES, 4)),
            pltpu.SemaphoreType.DMA((2,)),
        ],
        compiler_params=pltpu.CompilerParams(
            collective_id=0, has_side_effects=True, vmem_limit_bytes=48 * 2**20
        ),
        name="hubbard",
    )(
        band_coeffs.T,
        beta_vectors,
        atomic_waves,
        ortho_inverse,
        beta_coupling.T,
        hubbard_energy[None, :],
        band_weight[None, :],
        orbital_start[None, :],
        orbital_species[None, :],
        beta_start[None, :],
    )
    return out.T


def solution(mesh):
    placed = (
        P("ga", "band"), P("ga", None), P("ga", None), P(), P(), P(), P("band"), P(), P(), P(),
    )
    return jax.shard_map(shards, mesh=mesh, in_specs=placed, out_specs=P("ga", "band"), check_vma=False)
```

```python
import functools

import jax
import jax.numpy as jnp
from jax import lax
from jax.experimental import pallas as pl
from jax.experimental.pallas import tpu as pltpu
from jax.sharding import PartitionSpec as P

ORB_REACH = 4
BETA_REACH = 5
NY = 8
NZ = 16
CROSS_B = 2
CROSS_O = 2
MESH = pl.DeviceIdType.MESH
F32 = jnp.float32
BF16 = jnp.bfloat16


def dot_nn(a, b):
    return jnp.dot(a, b, preferred_element_type=F32)


def dot_nt(a, b):
    return lax.dot_general(a, b, (((1,), (1,)), ((), ())), preferred_element_type=F32)


def ahead(x, k):
    n = x.shape[1]
    return x if k % n == 0 else pltpu.roll(x, (-k) % n, 1)


def order(n):
    return sorted(range(1, n), key=lambda d: -min(d, n - d))


def wait_bytes(ref, sem):
    pltpu.make_async_copy(ref, ref, sem).wait()


class CrossSum:
    def __init__(self, src, dst, z_in, y_in, mine, sems, y, z, band):
        self.src, self.dst = src, dst
        self.z_in, self.y_in, self.mine = z_in, y_in, mine
        self.width = z_in.shape[2]
        self.tiles = self.width // 128
        self.base = src.shape[1] - 2 * self.width
        self.in_z, self.in_y, self.out_y, self.out_z = (sems[0].at[p] for p in range(4))
        self.sent = sems[1]
        self.y, self.z, self.band = y, z, band
        self.owners = [t * NY // self.tiles for t in range(self.tiles)]

    def place(self, z):
        rows = pl.ds(pl.multiple_of((z // 2) * 8, 8), 8)
        return rows, pl.ds(pl.multiple_of(self.base + (z % 2) * self.width, 128), self.width)

    def tile(self, t):
        rows, _ = self.place(self.z)
        return rows, pl.ds(pl.multiple_of(self.base + (self.z % 2) * self.width + t * 128, 128), 128)

    def copy(self, src, dst, recv, phase, y, z):
        pltpu.make_async_remote_copy(
            src_ref=src,
            dst_ref=dst,
            send_sem=self.sent.at[phase],
            recv_sem=recv,
            device_id=(y * NZ + z, self.band),
            device_id_type=MESH,
        ).start()

    def start(self):
        for d in order(NZ):
            to = (self.z + d) % NZ
            self.copy(self.src.at[self.place(to)], self.z_in.at[d - 1], self.in_z, 0, self.y, to)

    def sum_z(self):
        wait_bytes(self.z_in, self.in_z)
        total = self.src[self.place(self.z)]
        for d in range(NZ - 1):
            total = total + self.z_in[d]
        self.mine[...] = total
        for t, owner in enumerate(self.owners):

            def go(t=t, owner=owner):
                slot = (owner - self.y + NY) % NY - 1
                self.copy(self.mine.at[:, pl.ds(t * 128, 128)], self.y_in.at[slot], self.in_y, 1, owner, self.z)

            pl.when(self.y != owner)(go)

    def sum_y(self):
        for t, owner in enumerate(self.owners):

            def go(t=t):
                wait_bytes(self.y_in, self.in_y)
                total = self.mine[:, t * 128 : t * 128 + 128]
                for d in range(NY - 1):
                    total = total + self.y_in[d]
                here = self.tile(t)
                self.dst[here] = total
                at = self.dst.at[here]
                for d in order(NY):
                    self.copy(at, at, self.out_y, 2, (self.y + d) % NY, self.z)

            pl.when(self.y == owner)(go)

    def others(self, sem):
        owns = self.y == self.owners[0]
        for owner in self.owners[1:]:
            owns = jnp.logical_or(owns, self.y == owner)
        pl.when(owns)(lambda: wait_bytes(self.y_in.at[pl.ds(0, self.tiles - 1)], sem))
        pl.when(jnp.logical_not(owns))(lambda: wait_bytes(self.y_in.at[pl.ds(0, self.tiles)], sem))
        return owns

    def spread(self):
        self.others(self.out_y)
        at = self.dst.at[self.place(self.z)]
        for d in order(NZ):
            self.copy(at, at, self.out_z, 3, self.y, (self.z + d) % NZ)

    def finish(self):
        wait_bytes(self.z_in, self.out_z)

    def drain(self):
        wait_bytes(self.z_in, self.sent.at[0])
        owns = self.others(self.sent.at[1])
        pl.when(owns)(lambda: wait_bytes(self.y_in, self.sent.at[2]))
        wait_bytes(self.z_in, self.sent.at[3])


class RingSum:
    def __init__(self, src, dst, y_in, z_in, mine, sems, y, z, band):
        self.src, self.dst = src, dst
        self.pairs = y_in.shape[0]
        self.stride = NZ // self.pairs
        self.y_in, self.z_in, self.mine = y_in, z_in, mine
        self.in_y, self.in_z, self.out_z, self.out_y, self.sent = sems
        self.y, self.z, self.band = y, z, band
        self.home = (z // self.stride) % self.pairs
        near = sorted(range(self.pairs), key=lambda d: min(d, self.pairs - d))
        self.near = [(self.home + d) % self.pairs for d in near]
        self.rows = pl.ds(pl.multiple_of(y * 8, 8), 8)
        self.side = z % self.stride
        self.every = self.stride * self.pairs == NZ
        self.owner = jnp.logical_and(self.side < 2, z // self.stride < self.pairs)

    def lanes(self, pair):
        return pl.ds(pl.multiple_of(pair * 256, 256), 256)

    def tile(self, pair, side):
        return pl.ds(pl.multiple_of(pair * 256 + side * 128, 128), 128)

    def copy(self, src, dst, recv, phase, y, z):
        pltpu.make_async_remote_copy(
            src_ref=src,
            dst_ref=dst,
            send_sem=self.sent.at[phase],
            recv_sem=recv,
            device_id=(y * NZ + z, self.band),
            device_id_type=MESH,
        ).start()

    def when(self, cond, body):
        if self.every:
            body()
        else:
            pl.when(cond)(body)

    def unless(self, cond, body):
        if not self.every:
            pl.when(jnp.logical_not(cond))(body)

    def start(self, i):
        pair = self.near[self.pairs - 1 - i]
        for d in order(NY):
            to = (self.y + d) % NY
            rows = pl.ds(pl.multiple_of(to * 8, 8), 8)
            self.copy(self.src.at[rows, self.lanes(pair)], self.y_in.at[pair, d - 1], self.in_y.at[pair], 0, to, self.z)

    def sum_in(self):
        for i in range(self.pairs):
            pair = self.near[self.pairs - 1 - i]
            wait_bytes(self.y_in.at[pair], self.in_y.at[pair])
            total = self.src[self.rows, self.lanes(pair)]
            for d in range(NY - 1):
                total = total + self.y_in[pair, d]
            self.mine[:, self.lanes(pair)] = total
            for side in range(2):
                to = pair * self.stride + side

                def go(to=to, side=side, pair=pair):
                    gap = (to - self.z + NZ) % NZ - 1
                    self.copy(self.mine.at[:, self.tile(pair, side)], self.z_in.at[gap], self.in_z, 1, self.y, to)

                if i < self.pairs - 1 and self.every:
                    go()
                else:
                    pl.when(to != self.z)(go)

    def sum_out(self):
        def go():
            wait_bytes(self.z_in, self.in_z)
            here = self.tile(self.home, self.side)
            total = self.mine[:, here]
            for d in range(NZ - 1):
                total = total + self.z_in[d]
            self.dst[self.rows, here] = total
            at = self.dst.at[self.rows, here]
            for d in order(NZ):
                self.copy(at, at, self.out_z.at[self.home], 2, self.y, (self.z + d) % NZ)

        self.when(self.owner, go)

    def spread(self, low, high):
        for i in range(low, high):
            pair = self.near[i]
            sem = self.out_z.at[pair]
            at = self.dst.at[self.rows, self.lanes(pair)]
            if i == 0:
                self.when(self.owner, lambda: wait_bytes(self.z_in.at[0], sem))
                self.unless(self.owner, lambda: wait_bytes(self.z_in.at[pl.ds(0, 2)], sem))
            else:
                wait_bytes(self.z_in.at[pl.ds(0, 2)], sem)
            for d in order(NY):
                self.copy(at, at, self.out_y, 3, (self.y + d) % NY, self.z)

    def finish(self):
        wait_bytes(self.y_in, self.out_y)

    def drain(self):
        tiles = 2 * self.pairs
        wait_bytes(self.y_in, self.sent.at[0])
        if self.every:
            wait_bytes(self.z_in, self.sent.at[1])
        else:
            own = self.owner
            pl.when(own)(lambda: wait_bytes(self.z_in.at[pl.ds(0, tiles - 1)], self.sent.at[1]))
            pl.when(jnp.logical_not(own))(lambda: wait_bytes(self.z_in.at[pl.ds(0, tiles)], self.sent.at[1]))
        self.when(self.owner, lambda: wait_bytes(self.z_in, self.sent.at[2]))
        wait_bytes(self.y_in, self.sent.at[3])


def split3(x):
    high = x.astype(BF16)
    rest = x - high.astype(F32)
    mid = rest.astype(BF16)
    low = (rest - mid.astype(F32)).astype(BF16)
    return jnp.concatenate([high, mid, low], axis=0)


def kernel(
    psi_hbm, beta_hbm, atom_hbm, ortho_hbm, coup_hbm, energy_hbm, weight_hbm, ostart_hbm, ospec_hbm, bstart_hbm, out,
    psi, beta, atom, ortho, coup_in, energy, weight_in, ostart, ospec, bstart, coup, orb, wcol, wb, wo, fb, fo, half_b,
    half_o, hw, cpsi, pot, occ_mine, occ_in, yb_in, yo_in, z_in, mine_b, mine_o, xzb_in, xzo_in, xy_in, xmine_b, xmine_o,
    load_sem, piece_sem, in_y, in_z, out_z, out_y, sent, cross_in, cross_sent, occ_sem,
):
    bands, npw = psi.shape
    nbeta, norb = beta.shape[1], atom.shape[1]
    g = lax.axis_index("ga")
    band = lax.axis_index("band")
    y, z = g // NZ, g % NZ
    nband = 8

    def ring(which):
        if which == 1:
            src, dst, y_in, mine = wo, fo, yo_in, mine_o
        else:
            n = which // 2
            src, dst, y_in, mine = wb.at[n], fb.at[n], yb_in.at[n], mine_b.at[n]
        sems = (in_y.at[which], in_z.at[which], out_z.at[which], out_y.at[which], sent.at[which])
        x_in, x_mine = (xzo_in, xmine_o) if which == 1 else (xzb_in.at[which // 2], xmine_b.at[which // 2])
        x_sems = (cross_in.at[which], cross_sent.at[which])
        return (
            RingSum(src, dst, y_in, z_in.at[which], mine, sems, y, z, band),
            CrossSum(src, dst, x_in, xy_in.at[which], x_mine, x_sems, y, z, band),
        )

    (first_sum, first_cross), (second_sum, second_cross), (third_sum, third_cross) = ring(0), ring(1), ring(2)

    def carry(one, cross):
        one.sum_in()
        cross.sum_z()
        one.sum_out()
        cross.sum_y()
        one.spread(0, 1)
        cross.spread()
        one.spread(1, one.pairs)

    def pieces(one, cross):
        for first in range(cross.base, cross.base + 2 * cross.width, 256):
            yield pl.ds(first, 256), None
        for i in range(one.pairs):
            yield one.lanes(one.near[one.pairs - 1 - i]), i

    def begin(one, cross, i):
        if i is not None:
            if i == 0:
                cross.start()
            one.start(i)

    psi_load = pltpu.make_async_copy(psi_hbm, psi, load_sem.at[0])
    psi_load.start()
    beta_loads = []
    for n, (cols, _) in enumerate(pieces(first_sum, first_cross)):
        beta_loads.append(pltpu.make_async_copy(beta_hbm.at[:, cols], beta.at[:, cols], piece_sem.at[n]))
    pairs = [
        (coup_hbm, coup_in), (energy_hbm, energy), (weight_hbm, weight_in), (ostart_hbm, ostart), (ospec_hbm, ospec),
        (bstart_hbm, bstart), (atom_hbm, atom), (ortho_hbm, ortho),
    ]
    late = [pltpu.make_async_copy(a, b, load_sem.at[1 + i]) for i, (a, b) in enumerate(pairs)]
    for c in beta_loads + late:
        c.start()

    barrier = pltpu.get_barrier_semaphore()
    for d in order(NZ):
        pl.semaphore_signal(barrier, inc=1, device_id=(y * NZ + (z + d) % NZ, band), device_id_type=MESH)
    for d in order(NY):
        pl.semaphore_signal(barrier, inc=1, device_id=(((y + d) % NY) * NZ + z, band), device_id_type=MESH)
    for d in range(1, nband):
        pl.semaphore_signal(barrier, inc=1, device_id=(g, (band + d) % nband), device_id_type=MESH)

    psi_load.wait()
    for n, (cols, i) in enumerate(pieces(first_sum, first_cross)):
        beta_loads[n].wait()
        wb[0, :, cols] = dot_nn(psi[...], beta[:, cols])
        if i == 0:
            pl.semaphore_wait(barrier, NZ - 1 + NY - 1 + nband - 1)
        begin(first_sum, first_cross, i)

    for c in late:
        c.wait()
    place = lax.broadcasted_iota(jnp.int32, (1, nbeta), 1)
    first = bstart[...].reshape(1, nbeta)
    for k in range(-BETA_REACH, BETA_REACH + 1):
        there = jnp.logical_and(place + k >= 0, place + k < nbeta)
        same = jnp.logical_and(ahead(first, k) == first, there)
        mirror = ahead(coup_in[BETA_REACH - k : BETA_REACH - k + 1, :], k)
        value = 0.5 * (coup_in[BETA_REACH + k : BETA_REACH + k + 1, :] + mirror)
        coup[BETA_REACH + k : BETA_REACH + k + 1, :] = jnp.where(same, value, 0.0)
    place = lax.broadcasted_iota(jnp.int32, (1, norb), 1)
    first = ostart[...].reshape(1, norb)
    for k in range(-ORB_REACH, ORB_REACH + 1):
        there = jnp.logical_and(place + k >= 0, place + k < norb)
        same = jnp.logical_and(ahead(first, k) == first, there)
        orb[ORB_REACH + k : ORB_REACH + k + 1, :] = jnp.where(same, 1.0, 0.0)
    species = ospec[...].reshape(1, norb)
    u = jnp.zeros((1, norb), F32)
    for s in range(3):
        u = u + jnp.where(species == s, energy[s], 0.0)
    orb[2 * ORB_REACH + 1 : 2 * ORB_REACH + 2, :] = u
    row = lax.broadcasted_iota(jnp.int32, (bands, bands), 0)
    col = lax.broadcasted_iota(jnp.int32, (bands, bands), 1)
    wcol[...] = jnp.sum(jnp.where(row == col, weight_in[...].reshape(1, bands), 0.0), axis=1, keepdims=True)

    def apply_q(full):
        for i in range(bands // 16):
            pair = []
            for j in range(2):
                x = full[i * 16 + j * 8 : i * 16 + j * 8 + 8, :]
                total = coup[BETA_REACH : BETA_REACH + 1, :] * x
                for k in range(-BETA_REACH, BETA_REACH + 1):
                    if k != 0:
                        total = total + coup[BETA_REACH + k : BETA_REACH + k + 1, :] * ahead(x, k)
                pair.append(total)
            half_b[i * 16 : i * 16 + 16, :] = jnp.concatenate(pair, axis=0).astype(BF16)

    block = 256

    carry(first_sum, first_cross)
    first_sum.finish()
    first_cross.finish()
    apply_q(fb.at[0])
    for j in range(npw // block):
        cols = pl.ds(j * block, block)
        value = psi[:, cols].astype(F32) + dot_nt(half_b[...], beta[cols, :])
        cpsi[:, cols] = value.astype(BF16)
    for cols, i in pieces(second_sum, second_cross):
        wo[:, cols] = dot_nn(cpsi[...], atom[:, cols])
        begin(second_sum, second_cross, i)
    carry(second_sum, second_cross)

    def times_ortho(x):
        stacked = split3(x)
        for j in range(norb // block):
            cols = pl.ds(j * block, block)
            y3 = dot_nt(stacked, ortho[cols, :])
            yield cols, y3[:bands] + y3[bands : 2 * bands] + y3[2 * bands :]

    second_sum.finish()
    second_cross.finish()
    for cols, value in times_ortho(fo[...]):
        pot[:, cols] = value
    accs = None
    for i in range(bands // 8):
        p = pot[i * 8 : i * 8 + 8, :]
        weighted = p * wcol[i * 8 : i * 8 + 8, :]
        terms = [weighted * ahead(p, k) for k in range(ORB_REACH + 1)]
        accs = terms if accs is None else [a + t for a, t in zip(accs, terms)]
    for k in range(ORB_REACH + 1):
        occ_mine[k : k + 1, :] = jnp.sum(accs[k], axis=0, keepdims=True)
    occ_mine[ORB_REACH + 1 :, :] = jnp.zeros((8 - ORB_REACH - 1, norb), F32)
    for d in range(1, nband):
        pltpu.make_async_remote_copy(
            src_ref=occ_mine,
            dst_ref=occ_in.at[d - 1],
            send_sem=occ_sem.at[0],
            recv_sem=occ_sem.at[1],
            device_id=(g, (band + d) % nband),
            device_id_type=MESH,
        ).start()
    wait_bytes(occ_in, occ_sem.at[1])
    occ = occ_mine[...]
    for d in range(nband - 1):
        occ = occ + occ_in[d]

    u = orb[2 * ORB_REACH + 1 : 2 * ORB_REACH + 2, :]
    potential = []
    for k in range(-ORB_REACH, ORB_REACH + 1):
        value = occ[abs(k) : abs(k) + 1, :]
        value = ahead(value, k) if k < 0 else value
        same = orb[ORB_REACH + k : ORB_REACH + k + 1, :]
        potential.append(u * ((0.5 if k == 0 else 0.0) - value * same) * same)

    mixed = []
    for i in range(bands // 8):
        x = pot[i * 8 : i * 8 + 8, :]
        total = potential[ORB_REACH] * x
        for k in range(-ORB_REACH, ORB_REACH + 1):
            if k != 0:
                total = total + potential[ORB_REACH + k] * ahead(x, k)
        mixed.append(total)
    for cols, value in times_ortho(jnp.concatenate(mixed, axis=0)):
        half_o[:, cols] = value.astype(BF16)
    for j in range(npw // block):
        cols = pl.ds(j * block, block)
        value = dot_nt(half_o[...], atom[cols, :])
        hw[:, cols] = value
        cpsi[:, cols] = value.astype(BF16)
    for cols, i in pieces(third_sum, third_cross):
        wb[1, :, cols] = dot_nn(cpsi[...], beta[:, cols])
        begin(third_sum, third_cross, i)
    carry(third_sum, third_cross)
    third_sum.finish()
    third_cross.finish()
    apply_q(fb.at[1])
    for j in range(npw // block):
        cols = pl.ds(j * block, block)
        value = hw[:, cols] + dot_nt(half_b[...], beta[cols, :])
        out[:, cols] = value.astype(BF16)

    for s in (first_sum, first_cross, second_sum, second_cross, third_sum, third_cross):
        s.drain()
    wait_bytes(occ_in, occ_sem.at[0])


def shards(
    band_coeffs, beta_vectors, atomic_waves, beta_coupling, ortho_inverse, hubbard_energy, band_weight, orbital_start,
    orbital_species, beta_start,
):
    npw, bands = band_coeffs.shape
    nbeta, norb = beta_vectors.shape[1], atomic_waves.shape[1]
    hbm = pl.BlockSpec(memory_space=pl.ANY)
    vmem = pl.BlockSpec(memory_space=pltpu.VMEM)
    out = pl.pallas_call(
        kernel,
        out_shape=jax.ShapeDtypeStruct((bands, npw), BF16),
        in_specs=[hbm] * 10,
        out_specs=vmem,
        scratch_shapes=[
            pltpu.VMEM((bands, npw), BF16),
            pltpu.VMEM((npw, nbeta), BF16),
            pltpu.VMEM((npw, norb), BF16),
            pltpu.VMEM((norb, norb), BF16),
            pltpu.VMEM(beta_coupling.shape[::-1], F32),
            pltpu.SMEM(hubbard_energy.shape, F32),
            pltpu.VMEM((bands,), F32),
            pltpu.VMEM((norb,), jnp.int32),
            pltpu.VMEM((norb,), jnp.int32),
            pltpu.VMEM((nbeta,), jnp.int32),
            pltpu.VMEM((16, nbeta), F32),
            pltpu.VMEM((16, norb), F32),
            pltpu.VMEM((bands, 1), F32),
            pltpu.VMEM((2, bands, nbeta), F32),
            pltpu.VMEM((bands, norb), F32),
            pltpu.VMEM((2, bands, nbeta), F32),
            pltpu.VMEM((bands, norb), F32),
            pltpu.VMEM((bands, nbeta), BF16),
            pltpu.VMEM((bands, norb), BF16),
            pltpu.VMEM((bands, npw), F32),
            pltpu.VMEM((bands, npw), BF16),
            pltpu.VMEM((bands, norb), F32),
            pltpu.VMEM((8, norb), F32),
            pltpu.VMEM((7, 8, norb), F32),
            pltpu.VMEM((2, nbeta // 256 - CROSS_B, NY - 1, 8, 256), F32),
            pltpu.VMEM((norb // 256 - CROSS_O, NY - 1, 8, 256), F32),
            pltpu.VMEM((3, NZ - 1, 8, 128), F32),
            pltpu.VMEM((2, 8, nbeta), F32),
            pltpu.VMEM((8, norb), F32),
            pltpu.VMEM((2, NZ - 1, 8, 128 * CROSS_B), F32),
            pltpu.VMEM((NZ - 1, 8, 128 * CROSS_O), F32),
            pltpu.VMEM((3, NY - 1, 8, 128), F32),
            pltpu.VMEM((2, 8, 128 * CROSS_B), F32),
            pltpu.VMEM((8, 128 * CROSS_O), F32),
            pltpu.SemaphoreType.DMA((9,)),
            pltpu.SemaphoreType.DMA((nbeta // 256,)),
            pltpu.SemaphoreType.DMA((3, nbeta // 256)),
            pltpu.SemaphoreType.DMA((3,)),
            pltpu.SemaphoreType.DMA((3, nbeta // 256)),
            pltpu.SemaphoreType.DMA((3,)),
            pltpu.SemaphoreType.DMA((3, 4)),
            pltpu.SemaphoreType.DMA((3, 4)),
            pltpu.SemaphoreType.DMA((3, 4)),
            pltpu.SemaphoreType.DMA((2,)),
        ],
        compiler_params=pltpu.CompilerParams(
            collective_id=0, has_side_effects=True, vmem_limit_bytes=60 * 2**20
        ),
        name="hubbard",
    )(
        band_coeffs.T,
        beta_vectors,
        atomic_waves,
        ortho_inverse,
        beta_coupling.T,
        hubbard_energy,
        band_weight,
        orbital_start,
        orbital_species,
        beta_start,
    )
    return out.T


def solution(mesh):
    placed = (
        P("ga", "band"), P("ga", None), P("ga", None), P(), P(), P(), P("band"), P(), P(), P(),
    )
    return jax.shard_map(shards, mesh=mesh, in_specs=placed, out_specs=P("ga", "band"), check_vma=False)
```
